256 devices in a mesh: dp: 8 (over x_lo, y), tensor: 32 (over z, x_hi, core).
Axes of the slice: x: 4 (x_hi: 2, x_lo: 2; x = x_hi * 2 + x_lo), y: 4, z: 8, core: 2. Of those that a mesh axis runs over, the one named last changes fastest.
Arguments:
- hidden: bfloat16 [1024, 53248], P('dp', 'tensor'), may hold values from -0.29882812 to 0.29882812
- upstream: bfloat16 [1024, 8192], P('dp'), may hold values from -6 to 6
- weight: bfloat16 [53248, 8192], P('tensor', 'dp'), may hold values from -0.0625 to 0.0625
- scales: float32 [416, 8192], P('tensor', 'dp'), may hold values from 0.3 to 3
- clip_mask: int32 [416, 8192], P('tensor', 'dp'), may hold values 0 or 1
- rot_block: float32 [13, 13], replicated, may hold values from -1.75 to 1.75
Outputs:
- grad_hidden: bfloat16 [1024, 53248], P('dp', 'tensor')
- grad_weight: bfloat16 [53248, 8192], P('tensor', 'dp')
- grad_scales: float32 [416, 8192], P('tensor', 'dp')
The draws below stay inside these ranges and needn't reach their ends.
All inputs are finite; a program needn't handle non-finite values. No bound on the sum of `clip_mask` on one device may be relied on, other than what follows from the above.
Results may differ from the reference program's by a relative error of at most 0.023.
Values may be sent and summed in bfloat16 or wider, within the bound.
A program may use at most 192 MiB of HBM per device.

```python
import math
import jax
import jax.numpy as jnp
from jax import lax

D = 8192
FF = 53248
HB = 128
GROUP = 128
TOKENS = 1024
BLOCKS = 13
GROUPS = 416
N_TENSOR = 32


def set_ends(array, rng, least, largest):
    shape = array.shape
    place = [jax.random.randint(jax.random.fold_in(rng, axis), (), 0, shape[axis]) for axis in range(len(shape))]
    array = array.at[tuple(place)].set(least)
    longest = shape.index(max(shape))
    place[longest] = (place[longest] + 1) % shape[longest]
    return array.at[tuple(place)].set(largest)


def block_scale(own_key, shape, shards, low, high):
    def one(dim, blocks):
        steps = jax.random.uniform(jax.random.fold_in(jax.random.fold_in(own_key, 6), dim), (blocks,), jnp.float32, low / len(shards), high / len(shards))
        return jnp.repeat(jnp.exp(steps), shape[dim] // blocks).reshape((-1,) + (1,) * (len(shape) - dim - 1))

    factor_of = one(*shards[0])
    for cut in shards[1:]:
        factor_of = factor_of * one(*cut)
    return factor_of


def gaussian(own_key, shape, scale, bound, shards=(), kind=jnp.bfloat16):
    entries = jax.random.normal(own_key, shape, jnp.float32) * scale
    if len(shards) > 0:
        entries = block_scale(own_key, shape, shards, -0.22, 0.18) * entries
    return jnp.clip(entries, min=-bound, max=bound).astype(kind)


def setup_inputs(seed: int = 0) -> dict:
    key_list = jax.random.split(jax.random.key(seed), 7)
    return {
        "hidden": gaussian(key_list[0], (TOKENS, FF), 0.05, 0.29882812, ((0, 8), (1, 32))),
        "upstream": gaussian(key_list[1], (TOKENS, D), 1.0, 6.0, ((0, 8),)),
        "weight": gaussian(key_list[2], (FF, D), D ** -0.5, 0.0625, ((0, 32), (1, 8))),
        "scales": jnp.clip(jnp.exp(math.log(3.0) - 2.3025851 * jax.random.uniform(key_list[3], (GROUPS, D), jnp.float32) ** block_scale(key_list[3], (GROUPS, D), ((0, 32), (1, 8)), -0.2, 0.2)), 0.3, 3.0),
        "clip_mask": set_ends((jax.random.randint(key_list[4], (GROUPS, D), 0, 4) < 3).astype(jnp.int32), jax.random.fold_in(key_list[4], 1), 0, 1),
        "rot_block": gaussian(key_list[5], (BLOCKS, BLOCKS), BLOCKS ** -0.5, 1.75, (), jnp.float32),
    }


def sign_table(size):
    index = jnp.arange(size, dtype=jnp.int32)
    both = index[:, None] & index[None, :]
    parity = jnp.zeros((size, size), jnp.int32)
    for shift_bit in range(max(size.bit_length() - 1, 0)):
        parity = parity ^ ((both >> shift_bit) & 1)
    return 1.0 - 2.0 * parity.astype(jnp.float32)


def reference(hidden, upstream, weight, scales, clip_mask, rot_block):
    high = lax.Precision.HIGHEST
    blocks = FF // (N_TENSOR * HB)
    width = FF // N_TENSOR
    inner = sign_table(HB)
    cross = sign_table(N_TENSOR)
    shaped = hidden.astype(jnp.float32).reshape(TOKENS, N_TENSOR, blocks, HB)
    first = jnp.einsum('ntkb,bd->ntkd', shaped, inner, precision=high)
    local = (jnp.einsum('ntkd,kc->ntcd', first, rot_block, precision=high) * (HB ** -0.5)).astype(jnp.bfloat16)
    rotated = jnp.einsum('ntcd,ts->nscd', local.astype(jnp.float32), cross, precision=high) * (N_TENSOR ** -0.5)
    rotated = rotated.astype(jnp.bfloat16).reshape(TOKENS, N_TENSOR, width).transpose(1, 0, 2)
    per_group = width // GROUP
    weight_parts = weight.reshape(N_TENSOR, width, D)
    scale_parts = scales.reshape(N_TENSOR, per_group, D)
    mask_parts = clip_mask.reshape(N_TENSOR, per_group, D)

    def one_shard(items):
        rows_rot, w_part, s_part, m_part = items
        w_wide = w_part.astype(jnp.float32).reshape(per_group, GROUP, D)
        quant = (w_wide * s_part[:, None, :]).reshape(width, D).astype(jnp.bfloat16)
        grad = jnp.dot(rows_rot.T, upstream, preferred_element_type=jnp.float32).reshape(per_group, GROUP, D)
        g_weight = (m_part.astype(jnp.float32)[:, None, :] * s_part[:, None, :] * grad).reshape(width, D).astype(jnp.bfloat16)
        g_scale = jnp.sum(grad * w_wide, axis=1)
        g_rot = jnp.dot(upstream, quant.T, preferred_element_type=jnp.float32).astype(jnp.bfloat16)
        return g_weight, g_scale, g_rot

    g_weight, g_scale, g_rot = lax.map(one_shard, (rotated, weight_parts, scale_parts, mask_parts))
    grad_weight = g_weight.reshape(FF, D)
    grad_scales = g_scale.reshape(FF // GROUP, D)
    g_rot = g_rot.transpose(1, 0, 2).reshape(TOKENS, N_TENSOR, blocks, HB).astype(jnp.float32)
    mixed = (jnp.einsum('nscd,ts->ntcd', g_rot, cross, precision=high) * (N_TENSOR ** -0.5)).astype(jnp.bfloat16)
    back = jnp.einsum('ntcd,bd->ntcb', mixed.astype(jnp.float32), inner, precision=high)
    grad_hidden = (jnp.einsum('ntcb,kc->ntkb', back, rot_block, precision=high) * (HB ** -0.5)).astype(jnp.bfloat16)
    return grad_hidden.reshape(TOKENS, FF), grad_weight, grad_scales
```

```python
import jax
import jax.numpy as jnp
import numpy as np
from jax import lax
from jax.experimental import pallas as pl
from jax.experimental.pallas import tpu as pltpu
from jax.sharding import PartitionSpec as P

MESH = pl.DeviceIdType.MESH
BF = jnp.bfloat16
F32 = jnp.float32
HB = 128
NC = 13
W = NC * HB
E = 1024
CHUNKS = ((0, 768), (768, 1664))
N_SEM = 160


def sign_matrix(size):
    table = np.ones((1, 1), np.float32)
    while table.shape[0] < size:
        table = np.block([[table, table], [table, -table]])
    return table


def kernel(
    h_ref, up_hbm, w_hbm, sc_ref, mk_ref, rot_ref, s128_ref, k8_ref,
    gh_hbm, gw_hbm, gs_ref,
    w_v, wq, up, first, loc, loc_in, u, z_in, z_out, wz, xa, xa_send, rot, rot_t,
    part, r1, r2, t_in, comp, x_in, g, g_in, gu, gz_in, gz_out, mixed, gh_v, acc, gw_v,
    ssem, rsem, lsem,
):
    dp, tensor = lax.axis_index("dp"), lax.axis_index("tensor")
    xl, y = dp // 4, dp % 4
    z, xh, c = tensor // 4, (tensor // 2) % 2, tensor % 2
    sign_c = (1 - 2 * c).astype(F32)
    sign_x = (1 - 2 * xh).astype(F32)
    count = [0]

    def y_dev(d):
        return (xl * 4 + (y + d) % 4, tensor)

    def x_dev(q, d=0):
        return ((1 - xl) * 4 + (y + d) % 4, z * 4 + ((xh + q) % 2) * 2 + c)

    def z_dev(k):
        return (dp, ((z + k) % 8) * 4 + xh * 2 + c)

    core_dev = (dp, z * 4 + xh * 2 + (1 - c))

    def send(src, dst, dev):
        i = count[0]
        count[0] += 1
        cp = pltpu.make_async_remote_copy(
            src_ref=src, dst_ref=dst, send_sem=ssem.at[i], recv_sem=rsem.at[i],
            device_id=dev, device_id_type=MESH,
        )
        cp.start()
        sent.append(cp)
        return cp

    sent = []

    def rows(start, size, step):
        return pl.ds(pl.multiple_of(start, step), size)

    def by_cols(c0, c1, body):
        @pl.loop(c0 // HB, c1 // HB)
        def _(i):
            body(pl.ds(pl.multiple_of(i * HB, HB), HB))

    def wide(ref, *at):
        return ref[at].astype(F32)

    w_load = pltpu.make_async_copy(w_hbm, w_v, lsem.at[0])
    w_load.start()
    own_up = pltpu.make_async_copy(
        up_hbm.at[:, pl.ds(pl.multiple_of(dp * E, E), E)], up.at[pl.ds(0, HB)], lsem.at[1]
    )
    own_up.start()
    peers = [y_dev(d) for d in (1, 2, 3)] + [x_dev(q, d) for d in range(4) for q in range(2)]
    peers += [z_dev(k) for k in range(1, 8)] + [core_dev]
    barrier = pltpu.get_barrier_semaphore()
    for dev in peers:
        pl.semaphore_signal(barrier, inc=1, device_id=dev, device_id_type=MESH)
    pl.semaphore_wait(barrier, len(peers))

    up_cp = {}
    for d in (2, 1, 3, 0):
        if d:
            to = xl * 4 + (y + d) % 4
            at = rows(c * 64, 64, 64)
            up_cp[(4 - d) % 4, 0] = [
                send(
                    up_hbm.at[at, pl.ds(pl.multiple_of(to * E, E), E)],
                    up.at[rows(((4 - d) % 4) * 256 + c * 64, 64, 64)],
                    y_dev(d),
                )
            ]
        to = (1 - xl) * 4 + (y + d) % 4
        at = rows(c * 64 + xh * 32, 32, 32)
        up_cp[(4 - d) % 4, 1] = [
            send(
                up_hbm.at[at, pl.ds(pl.multiple_of(to * E, E), E)],
                up.at[rows(((4 - d) % 4) * 256 + HB + c * 64 + xh * 32, 32, 32)],
                x_dev(q, d),
            )
            for q in range(2)
        ]

    def share_up(d):
        shared = []
        for xr in range(2):
            if (d, xr) == (0, 0):
                continue
            for cp in up_cp[d, xr]:
                cp.wait_recv()
            block = up.at[rows(d * 256 + xr * HB + c * 64, 64, 64)]
            shared.append(send(block, block, core_dev))
        return shared

    def local(src, dst, coef):
        @pl.loop(0, NC)
        def _(k):
            at = pl.ds(pl.multiple_of(k * HB, HB), HB)
            first[k] = jnp.dot(src[:, at], s128_ref[...], preferred_element_type=F32)

        @pl.loop(0, 4)
        def _(i):
            at = rows(i * 32, 32, 32)
            parts = [first[k, at, :] for k in range(NC)]
            for o in range(NC):
                total = parts[0] * coef(0, o)
                for k in range(1, NC):
                    total = total + parts[k] * coef(k, o)
                dst[at, o * HB : (o + 1) * HB] = (total * HB**-0.5).astype(BF)

    local(h_ref, loc, lambda k, o: rot_ref[k, o])
    core_a = send(loc, loc_in, core_dev)

    w_load.wait()

    @pl.loop(0, NC)
    def _(i):
        at = rows(i * HB, HB, HB)
        wq[at, :] = (w_v[at, :].astype(F32) * sc_ref[pl.ds(i, 1), :]).astype(BF)

    def z_start(src, dst, cols):
        at = rows(z * 16, 16, 16)
        cps = [
            send(src.at[rows(((z + k) % 8) * 16, 16, 16), cols], dst.at[at, cols], z_dev(k))
            for k in (4, 3, 5, 2, 6, 1, 7)
        ]
        dst[at, cols] = src[at, cols]
        return cps

    def z_mix(src, dst, c0, c1):
        def body(at):
            mix = jnp.dot(k8_ref[...], src[:, at], preferred_element_type=F32)
            dst[:, at] = (mix * 32.0**-0.5).astype(BF)

        by_cols(c0, c1, body)

    def recv(cps):
        for cp in cps:
            cp.wait_recv()

    core_a.wait_recv()

    def body(at):
        u[:, at] = (wide(loc, slice(None), at) * sign_c + wide(loc_in, slice(None), at)).astype(BF)

    by_cols(0, W, body)
    za = z_start(u, z_in, slice(0, W))

    def multiply(d, c0, c1):
        def tile(at):
            r = lax.dot_general(
                up[d * 256 : (d + 1) * 256, :], wq[at, :], (((1,), (1,)), ((), ())),
                preferred_element_type=F32,
            )
            part[d, :, at] = r.astype(BF)

        @pl.loop(c0 // 256, c1 // 256)
        def _(i):
            tile(pl.ds(pl.multiple_of(i * 256, 256), 256))

        if c1 % 256:
            tile(slice(c1 - HB, c1))

    r1_cp, r2_cp = {}, {}

    def y_first(j):
        cols = slice(*CHUNKS[j])
        r1_cp[j] = [
            send(part.at[2, pl.ds(0, HB), cols], r1.at[0, :, cols], y_dev(1)),
            send(part.at[2, pl.ds(HB, HB), cols], r1.at[1, :, cols], y_dev(3)),
        ]

    def y_direct(j):
        cols = slice(*CHUNKS[j])
        r2_cp[j] = [
            send(part.at[1, pl.ds(HB, HB), cols], r2.at[0, pl.ds(HB, HB), cols], y_dev(1)),
            send(part.at[3, pl.ds(0, HB), cols], r2.at[1, pl.ds(0, HB), cols], y_dev(3)),
        ]

    def y_second(j):
        cols = slice(*CHUNKS[j])
        recv(r1_cp[j])

        def body(at):
            lo, hi = slice(0, HB), slice(HB, 256)
            part[1, lo, at] = (wide(part, 1, lo, at) + wide(r1, 0, slice(None), at)).astype(BF)
            part[3, hi, at] = (wide(part, 3, hi, at) + wide(r1, 1, slice(None), at)).astype(BF)

        by_cols(*CHUNKS[j], body)
        r2_cp[j] += [
            send(part.at[1, pl.ds(0, HB), cols], r2.at[0, pl.ds(0, HB), cols], y_dev(1)),
            send(part.at[3, pl.ds(HB, HB), cols], r2.at[1, pl.ds(HB, HB), cols], y_dev(3)),
        ]

    t_cp, x_cp, g_cp, gz_cp, gw_cp = {}, {}, {}, {}, {}

    def x_first(j):
        cols = slice(*CHUNKS[j])
        recv(r2_cp[j])

        def body(at):
            part[0, :, at] = (
                wide(part, 0, slice(None), at) + wide(r2, 0, slice(None), at) + wide(r2, 1, slice(None), at)
            ).astype(BF)

        by_cols(*CHUNKS[j], body)
        t_cp[j] = [
            send(part.at[0, rows(((xh + q) % 2) * 64, 64, 64), cols], t_in.at[q, :, cols], x_dev(q))
            for q in range(2)
        ]
        x_cp[j] = [
            send(
                part.at[0, rows(HB + (1 - xh) * 64, 64, 64), cols],
                x_in.at[q, rows((1 - xh) * 64, 64, 64), cols],
                x_dev(q),
            )
            for q in range(2)
        ]

    def x_second(j):
        cols = slice(*CHUNKS[j])
        recv(t_cp[j])

        def body(at):
            own = wide(part, 0, rows(HB + xh * 64, 64, 64), at)
            comp[0, :, at] = (own * sign_x + wide(t_in, 1, slice(None), at)).astype(BF)
            comp[1, :, at] = (own + wide(t_in, 0, slice(None), at)).astype(BF)

        by_cols(*CHUNKS[j], body)
        x_cp[j] += [
            send(comp.at[q, :, cols], x_in.at[q, rows(xh * 64, 64, 64), cols], x_dev(q)) for q in range(2)
        ]

    def core_first(j):
        cols = slice(*CHUNKS[j])
        recv(x_cp[j])

        def body(at):
            near, far = rows(xh * 64, 64, 64), rows((1 - xh) * 64, 64, 64)
            g[near, at] = (
                wide(part, 0, near, at) * sign_x + wide(x_in, 0, near, at) + wide(x_in, 1, near, at)
            ).astype(BF)
            g[far, at] = (
                (wide(part, 0, far, at) + wide(x_in, 0, far, at)) * sign_x + wide(x_in, 1, far, at)
            ).astype(BF)

        by_cols(*CHUNKS[j], body)
        g_cp[j] = send(g.at[:, cols], g_in.at[:, cols], core_dev)

    def core_second(j):
        g_cp[j].wait_recv()

        def body(at):
            gu[:, at] = (wide(g, slice(None), at) * sign_c + wide(g_in, slice(None), at)).astype(BF)

        by_cols(*CHUNKS[j], body)
        gz_cp[j] = z_start(gu, gz_in, slice(*CHUNKS[j]))

    def z_second(j):
        recv(gz_cp[j])
        z_mix(gz_in, gz_out, *CHUNKS[j])
        gw_cp[j] = z_start(gz_out, mixed, slice(*CHUNKS[j]))

    def turn(d):
        at_t = slice(d * 256, (d + 1) * 256)

        @pl.loop(0, NC)
        def _(i):
            at = rows(i * HB, HB, HB)
            rot_t[at, at_t] = rot[at_t, at].T

    def add_grad(d, at, fresh):
        own = slice(d * 256, (d + 1) * 256)
        term = jnp.dot(rot_t[:, own], up[own, at], preferred_element_type=F32)
        acc[:, at] = term if fresh else acc[:, at] + term

    def grad_step(d, fresh=False):
        turn(d)

        @pl.loop(0, 4)
        def _(i):
            add_grad(d, rows(i * 256, 256, 256), fresh)

    def rot_slot(d, xr, at=slice(None)):
        return rot.at[pl.ds(d * 256 + xr * HB, HB)]

    def rot_part(d, xr, lo):
        return rot.at[pl.ds(d * 256 + xr * HB + lo, 64)]

    def gather_first(xr):
        return {
            3: send(rot_slot(0, xr), rot_slot(3, xr), y_dev(1)),
            1: send(rot_slot(0, xr), rot_slot(1, xr), y_dev(3)),
        }

    def gather_second(cps, xr):
        cps[3].wait_recv()
        one = send(rot_part(3, xr, 0), rot_part(2, xr, 0), y_dev(1))
        cps[1].wait_recv()
        two = send(rot_part(1, xr, 64), rot_part(2, xr, 64), y_dev(3))
        return [one, two]

    shared = share_up(2)
    recv(shared)
    multiply(2, 0, W)
    y_first(0)
    shared = share_up(1) + share_up(3)
    recv(shared)
    multiply(1, 0, W)
    multiply(3, 0, W)
    y_direct(0)
    y_first(1)
    shared = share_up(0)

    recv(za)
    z_mix(z_in, z_out, 0, W)
    zb = z_start(z_out, wz, slice(0, W))

    recv(shared)
    own_up.wait()
    multiply(0, 0, W)
    y_second(0)
    y_direct(1)

    recv(zb)
    xa_cp = [send(wz, xa.at[q], x_dev(q)) for q in range(2)]
    x_first(0)
    y_second(1)
    x_second(0)
    recv(xa_cp)

    def body(at):
        a0, a1 = wide(xa, 0, slice(None), at), wide(xa, 1, slice(None), at)
        rot[HB:256, at] = (a0 * sign_x + a1).astype(BF)
        xa_send[:, at] = (a0 - a1 * sign_x).astype(BF)

    by_cols(0, W, body)
    half = rows(xh * 64, 64, 64)
    xb_cp = [
        send(rot.at[rows(HB + xh * 64, 64, 64)], rot.at[half], x_dev(0)),
        send(xa_send.at[half], rot.at[half], x_dev(1)),
    ]
    far_cp = gather_first(1)
    core_first(0)
    core_second(0)
    x_first(1)
    recv(xb_cp)
    near_cp = gather_first(0)
    x_second(1)
    z_second(0)
    grad_step(0, True)
    core_first(1)
    core_second(1)
    last = gather_second(far_cp, 1)
    z_second(1)
    last += gather_second(near_cp, 0)
    grad_step(1)
    grad_step(3)
    recv(gw_cp[0])
    recv(gw_cp[1])
    local(mixed, gh_v, lambda k, o: rot_ref[o, k])
    gh_out = pltpu.make_async_copy(gh_v, gh_hbm, lsem.at[2])
    gh_out.start()

    recv(last)
    turn(2)
    outs = []
    for i in range(4):
        at = slice(i * 256, (i + 1) * 256)
        add_grad(2, at, False)

        @pl.loop(0, NC)
        def _(k):
            group = rows(k * HB, HB, HB)
            one = pl.ds(k, 1)
            grad = acc[group, at]
            gs_ref[one, at] = jnp.sum(grad * w_v[group, at].astype(F32), axis=0, keepdims=True)
            gw_v[group, at] = (grad * (sc_ref[one, at] * mk_ref[one, at].astype(F32))).astype(BF)

        outs.append(pltpu.make_async_copy(gw_v.at[:, at], gw_hbm.at[:, at], lsem.at[3 + i]))
        outs[-1].start()
    for cp in outs:
        cp.wait()
    gh_out.wait()
    for cp in sent:
        cp.wait_send()


def solution(mesh):
    def step(hidden, upstream, weight, scales, clip_mask, rot_block):
        s128 = jnp.asarray(sign_matrix(HB), BF)
        k8 = jnp.asarray(np.kron(sign_matrix(8), np.eye(16, dtype=np.float32)), BF)
        vmem = pl.BlockSpec(memory_space=pltpu.VMEM)
        smem = pl.BlockSpec(memory_space=pltpu.SMEM)
        anywhere = pl.BlockSpec(memory_space=pl.ANY)
        full = pltpu.VMEM((HB, W), BF)
        two = pltpu.VMEM((2, HB, W), BF)
        tall = pltpu.VMEM((8 * HB, W), BF)
        wide = pltpu.VMEM((W, E), BF)
        scratch = [
            wide, wide, pltpu.VMEM((8 * HB, E), BF), pltpu.VMEM((NC, HB, HB), F32),
            full, full, full, full, full, full, two, full, tall, wide,
            pltpu.VMEM((4, 2 * HB, W), BF), two, pltpu.VMEM((2, 2 * HB, W), BF),
            pltpu.VMEM((2, 64, W), BF), pltpu.VMEM((2, 64, W), BF), two,
            full, full, full, full, full, full, full, pltpu.VMEM((W, E), F32), wide,
            pltpu.SemaphoreType.DMA((N_SEM,)), pltpu.SemaphoreType.DMA((N_SEM,)), pltpu.SemaphoreType.DMA((8,)),
        ]
        return pl.pallas_call(
            kernel,
            name="fused",
            out_shape=(
                jax.ShapeDtypeStruct((HB, W), BF),
                jax.ShapeDtypeStruct((W, E), BF),
                jax.ShapeDtypeStruct((NC, E), F32),
            ),
            in_specs=[vmem, anywhere, anywhere, vmem, vmem, smem, vmem, vmem],
            out_specs=(anywhere, anywhere, vmem),
            scratch_shapes=scratch,
            compiler_params=pltpu.CompilerParams(
                collective_id=0, has_side_effects=True, vmem_limit_bytes=56 * 2**20
            ),
        )(hidden, upstream, weight, scales, clip_mask, rot_block, s128, k8)

    return jax.shard_map(
        step,
        mesh=mesh,
        in_specs=(
            P("dp", "tensor"),
            P("dp", None),
            P("tensor", "dp"),
            P("tensor", "dp"),
            P("tensor", "dp"),
            P(),
        ),
        out_specs=(P("dp", "tensor"), P("tensor", "dp"), P("tensor", "dp")),
        check_vma=False,
    )
```

```python
import jax
import jax.numpy as jnp
import numpy as np
from jax import lax
from jax.experimental import pallas as pl
from jax.experimental.pallas import tpu as pltpu
from jax.sharding import PartitionSpec as P

MESH = pl.DeviceIdType.MESH
BF = jnp.bfloat16
F32 = jnp.float32
HB = 128
NC = 13
W = NC * HB
E = 1024
CHUNKS = ((0, 768), (768, 1664))
OUT_ROWS = ((0, 896), (896, 1664))
PLACE = {0: 0, 1: 256, 3: 512, 2: 768}
N_SEM = 40


def sign_matrix(size):
    table = np.ones((1, 1), np.float32)
    while table.shape[0] < size:
        table = np.block([[table, table], [table, -table]])
    return table


def kernel(
    h_ref, up_hbm, w_hbm, sc_ref, mk_ref, rot_ref, s128_ref,
    gh_hbm, gw_hbm, gs_hbm,
    up_v, w_v, wq, up, first, loc, loc_in, u, z_in, z_out, wz, xa, xa_send, rot,
    part, r1, r2, t_in, comp, x_in, g, g_in, gu, gz_in, gz_out, mixed, gh_v, acc, gw_v, gs_ref,
    ssem, rsem, lsem,
):
    dp, tensor = lax.axis_index("dp"), lax.axis_index("tensor")
    xl, y = dp // 4, dp % 4
    z, xh, c = tensor // 4, (tensor // 2) % 2, tensor % 2
    sign_c = (1 - 2 * c).astype(F32)
    sign_x = (1 - 2 * xh).astype(F32)
    sent = []

    def y_dev(d):
        return (xl * 4 + (y + d) % 4, tensor)

    def x_dev(q, d=0):
        return ((1 - xl) * 4 + (y + d) % 4, z * 4 + ((xh + q) % 2) * 2 + c)

    def z_dev(k):
        return (dp, ((z + k) % 8) * 4 + xh * 2 + c)

    core_dev = (dp, z * 4 + xh * 2 + (1 - c))

    class Group:
        def __init__(self, like):
            self.like, self.i = like, len(sent)
            sent.append(self)

        def send(self, src, dst, dev):
            pltpu.make_async_remote_copy(
                src_ref=src, dst_ref=dst, send_sem=ssem.at[self.i], recv_sem=rsem.at[self.i],
                device_id=dev, device_id_type=MESH,
            ).start()
            return self

        def recv(self):
            pltpu.make_async_copy(self.like, self.like, rsem.at[self.i]).wait()

        def finish(self):
            pltpu.make_async_copy(self.like, self.like, ssem.at[self.i]).wait()

    def send(src, dst, dev):
        return Group(src).send(src, dst, dev)

    def rows(start, size, step):
        return pl.ds(pl.multiple_of(start, step), size)

    def wide(ref, *at):
        return ref[at].astype(F32)

    up_load = pltpu.make_async_copy(up_hbm, up_v, lsem.at[1])
    up_load.start()
    w_load = pltpu.make_async_copy(w_hbm, w_v, lsem.at[0])
    w_load.start()
    peers = [y_dev(d) for d in (1, 2, 3)] + [x_dev(q, d) for d in range(4) for q in range(2)]
    peers += [z_dev(k) for k in range(1, 8)] + [core_dev]
    barrier = pltpu.get_barrier_semaphore()
    for dev in peers:
        pl.semaphore_signal(barrier, inc=1, device_id=dev, device_id_type=MESH)

    def mix_blocks(store, coef):
        @pl.loop(0, 4)
        def _(i):
            at = rows(i * 32, 32, 32)
            parts = [first[k, at, :] for k in range(NC)]
            for o in range(NC):
                total = parts[0] * coef(0, o)
                for k in range(1, NC):
                    total = total + parts[k] * coef(k, o)
                store(i, o, (total * HB**-0.5).astype(BF))

    for k in range(NC):
        first[k] = lax.dot_general(
            s128_ref[...], h_ref[:, k * HB : (k + 1) * HB], (((1,), (1,)), ((), ())),
            preferred_element_type=F32,
        )

    def store_loc(i, o, value):
        loc[rows(o * HB + i * 32, 32, 32), :] = value

    mix_blocks(store_loc, lambda k, o: rot_ref[k, o])
    up_load.wait()
    pl.semaphore_wait(barrier, len(peers))

    up_cp = {}
    for d in (2, 1, 3, 0):
        slot_of = (4 - d) % 4
        there = PLACE[slot_of]
        up_cp[slot_of] = Group(up.at[pl.ds(there, HB if d else 64)])
        if d:
            to = xl * 4 + (y + d) % 4
            up_cp[slot_of].send(
                up_v.at[rows(c * 64, 64, 64), pl.ds(pl.multiple_of(to * E, E), E)],
                up.at[rows(there + c * 64, 64, 64)],
                y_dev(d),
            )
        to = (1 - xl) * 4 + (y + d) % 4
        quarter = c * 64 + xh * 32
        for q in range(2):
            up_cp[slot_of].send(
                up_v.at[rows(quarter, 32, 32), pl.ds(pl.multiple_of(to * E, E), E)],
                up.at[rows(there + HB + quarter, 32, 32)],
                x_dev(q, d),
            )
    core_a = send(loc, loc_in, core_dev)

    def share_up(d):
        up_cp[d].recv()
        shared = Group(up.at[pl.ds(PLACE[d], HB if d else 64)])
        for xr in range(0 if d else 1, 2):
            block = up.at[rows(PLACE[d] + xr * HB + c * 64, 64, 64)]
            shared.send(block, block, core_dev)
        return shared

    w_load.wait()

    @pl.loop(0, NC)
    def _(i):
        at = rows(i * HB, HB, HB)
        wq[at, :] = (w_v[at, :].astype(F32) * sc_ref[pl.ds(i, 1), :]).astype(BF)

    def z_start(src, dst, r0, r1_):
        b = (r1_ - r0) // 8
        at = rows(r0 + z * b, b, 16)
        group = Group(dst.at[pl.ds(r0, 7 * b)])
        for k in (4, 3, 5, 2, 6, 1, 7):
            group.send(src.at[rows(r0 + ((z + k) % 8) * b, b, 16)], dst.at[at], z_dev(k))
        dst[at, :] = src[at, :]
        return group

    def z_mix(src, dst, r0, r1_):
        b = (r1_ - r0) // 8

        @pl.loop(0, b // 16)
        def _(i):
            at = [rows(r0 + k * b + i * 16, 16, 16) for k in range(8)]
            v = [wide(src, at[k]) for k in range(8)]
            for bit in (1, 2, 4):
                v = [v[k ^ bit] - v[k] if k & bit else v[k] + v[k | bit] for k in range(8)]
            for k in range(8):
                dst[at[k], :] = (v[k] * 32.0**-0.5).astype(BF)

    core_a.recv()
    u[...] = (wide(loc, ...) * sign_c + wide(loc_in, ...)).astype(BF)
    za = [z_start(u, z_in, *rs) for rs in CHUNKS]

    def multiply(d):
        group = up[PLACE[d] : PLACE[d] + 256, :]
        r = lax.dot_general(wq[...], group, (((1,), (1,)), ((), ())), preferred_element_type=F32)
        for xr in range(2):
            part[d, xr] = r[:, xr * HB : (xr + 1) * HB].astype(BF)

    r1_cp, r2_cp = {}, {}

    def chunk(j):
        return pl.ds(CHUNKS[j][0], CHUNKS[j][1] - CHUNKS[j][0])

    def y_first(j):
        at = chunk(j)
        r1_cp[j] = [
            send(part.at[2, 0, at], r1.at[0, at], y_dev(1)),
            send(part.at[2, 1, at], r1.at[1, at], y_dev(3)),
        ]

    def y_direct(j):
        at = chunk(j)
        r2_cp[j] = Group(r2.at[:, :, at])
        r2_cp[j].send(part.at[1, 1, at], r2.at[0, 1, at], y_dev(1))
        r2_cp[j].send(part.at[3, 0, at], r2.at[1, 0, at], y_dev(3))

    def y_second(j):
        at = chunk(j)
        r1_cp[j][0].recv()
        part[1, 0, at] = (wide(part, 1, 0, at) + wide(r1, 0, at)).astype(BF)
        r2_cp[j].send(part.at[1, 0, at], r2.at[0, 0, at], y_dev(1))
        r1_cp[j][1].recv()
        part[3, 1, at] = (wide(part, 3, 1, at) + wide(r1, 1, at)).astype(BF)
        r2_cp[j].send(part.at[3, 1, at], r2.at[1, 1, at], y_dev(3))

    t_cp, x_cp, g_cp, gz_cp, gw_cp = {}, {}, {}, {}, {}

    def half(j, which):
        r0, r1_ = CHUNKS[j]
        return rows(r0 + which * ((r1_ - r0) // 2), (r1_ - r0) // 2, 64)

    def packed(j):
        r0, r1_ = CHUNKS[j]
        return pl.ds(r0 // 2, (r1_ - r0) // 2)

    def x_first(j):
        at = chunk(j)
        r2_cp[j].recv()
        for xr in range(2):
            total = wide(part, 0, xr, at) + wide(r2, 0, xr, at) + wide(r2, 1, xr, at)
            part[0, xr, at] = total.astype(BF)
        t_cp[j], x_cp[j] = Group(t_in.at[:, packed(j)]), Group(x_in.at[:, at])
        other = half(j, 1 - xh)
        for q in range(2):
            t_cp[j].send(part.at[0, 0, half(j, (xh + q) % 2)], t_in.at[q, packed(j)], x_dev(q))
        for q in range(2):
            x_cp[j].send(part.at[0, 1, other], x_in.at[q, other], x_dev(q))

    def x_second(j):
        mine, there = half(j, xh), packed(j)
        t_cp[j].recv()
        own = wide(part, 0, 1, mine)
        comp[0, there] = (own * sign_x + wide(t_in, 1, there)).astype(BF)
        comp[1, there] = (own + wide(t_in, 0, there)).astype(BF)
        for q in range(2):
            x_cp[j].send(comp.at[q, there], x_in.at[q, mine], x_dev(q))

    def core_first(j):
        x_cp[j].recv()
        near, far = half(j, xh), half(j, 1 - xh)
        g[near, :] = (wide(part, 0, 0, near) * sign_x + wide(x_in, 0, near) + wide(x_in, 1, near)).astype(BF)
        g[far, :] = ((wide(part, 0, 0, far) + wide(x_in, 0, far)) * sign_x + wide(x_in, 1, far)).astype(BF)
        g_cp[j] = send(g.at[chunk(j)], g_in.at[chunk(j)], core_dev)

    def core_second(j):
        at = chunk(j)
        g_cp[j].recv()
        gu[at, :] = (wide(g, at) * sign_c + wide(g_in, at)).astype(BF)
        gz_cp[j] = z_start(gu, gz_in, *CHUNKS[j])

    def z_second(j):
        gz_cp[j].recv()
        z_mix(gz_in, gz_out, *CHUNKS[j])
        gw_cp[j] = z_start(gz_out, mixed, *CHUNKS[j])

    def add_grad(slots, r0, r1_, fresh):
        tokens = slice(slots[0] * HB, (slots[-1] + 1) * HB)

        @pl.loop(0, 2)
        def _(i):
            columns = rows(i * 512, 512, 512)
            block = jnp.concatenate([rot[k, r0:r1_, :] for k in slots], axis=1)
            term = jnp.dot(block, up[tokens, columns], preferred_element_type=F32)
            acc[r0:r1_, columns] = term if fresh else acc[r0:r1_, columns] + term

    def grad_step(slots, fresh=False):
        for r0, r1_ in OUT_ROWS:
            add_grad(slots, r0, r1_, fresh)

    def slot(d, xr):
        return PLACE[d] // HB + xr

    def gather_first(xr):
        own = rot.at[slot(0, xr)]
        return send(own, rot.at[slot(3, xr)], y_dev(1)), send(own, rot.at[slot(1, xr)], y_dev(3))

    def gather_second(cps, xr):
        top, low = pl.ds(0, W // 2), pl.ds(W // 2, W // 2)
        cps[0].recv()
        one = send(rot.at[slot(3, xr), top], rot.at[slot(2, xr), top], y_dev(1))
        cps[1].recv()
        two = send(rot.at[slot(1, xr), low], rot.at[slot(2, xr), low], y_dev(3))
        return [one, two]

    zb = []
    def zret(j):
        za[j].recv()
        z_mix(z_in, z_out, *(CHUNKS[j] if len(za) == 2 else (0, W)))
        zb.append(z_start(z_out, wz, *(CHUNKS[j] if len(za) == 2 else (0, W))))
    xa_cp = Group(xa)
    def xa_start(j):
        zb[j].recv()
        at = chunk(j) if len(za) == 2 else pl.ds(0, W)
        for q in range(2):
            xa_cp.send(wz.at[at], xa.at[q, at], x_dev(q))
    def p0():
        shared.recv()
        up[0:HB, :] = up_v[:, pl.ds(pl.multiple_of(dp * E, E), E)]
        multiply(0)
    def xmid():
        xa_cp.recv()
        rot[slot(0, 1)] = (wide(xa, 0) * sign_x + wide(xa, 1)).astype(BF)
        xa_send[...] = (wide(xa, 0) - wide(xa, 1) * sign_x).astype(BF)
        own_half = rows(xh * (W // 2), W // 2, W // 2)
        xb_cp = Group(rot.at[slot(0, 0)])
        xb_cp.send(rot.at[slot(0, 1), own_half], rot.at[slot(0, 0), own_half], x_dev(0))
        xb_cp.send(xa_send.at[own_half], rot.at[slot(0, 0), own_half], x_dev(1))
        return xb_cp
    shared = share_up(2)
    shared.recv()
    multiply(2)
    y_first(0)
    shared = share_up(1), share_up(3)
    shared[0].recv()
    shared[1].recv()
    multiply(1)
    multiply(3)
    y_direct(0)
    y_first(1)
    shared = share_up(0)
    for j in range(len(za)): zret(j)
    p0()
    y_second(0)
    y_direct(1)
    for j in range(len(za)): xa_start(j)
    x_first(0)
    y_second(1)
    x_second(0)
    xb_cp = xmid()
    far_cp = gather_first(1)
    core_first(0)
    core_second(0)
    x_first(1)
    xb_cp.recv()
    near_cp = gather_first(0)
    x_second(1)
    z_second(0)
    grad_step((0, 1), True)
    core_first(1)
    core_second(1)
    last = gather_second(far_cp, 1)
    z_second(1)
    last += gather_second(near_cp, 0)
    grad_step((2, 3, 4, 5))
    gw_cp[0].recv()
    gw_cp[1].recv()
    for k in range(NC):
        first[k] = lax.dot_general(
            mixed[k * HB : (k + 1) * HB, :], s128_ref[...], (((0,), (0,)), ((), ())),
            preferred_element_type=F32,
        )

    def store_gh(i, o, value):
        gh_v[rows(i * 32, 32, 32), o * HB : (o + 1) * HB] = value

    mix_blocks(store_gh, lambda k, o: rot_ref[o, k])
    gh_out = pltpu.make_async_copy(gh_v, gh_hbm, lsem.at[2])
    gh_out.start()

    for cp in last:
        cp.recv()
    outs = []
    for i, (r0, r1_) in enumerate(OUT_ROWS):
        add_grad((6, 7), r0, r1_, False)

        @pl.loop(r0 // HB, r1_ // HB)
        def _(k):
            group = rows(k * HB, HB, HB)
            one = pl.ds(k, 1)
            for at in (slice(0, 512), slice(512, 1024)):
                grad = acc[group, at]
                gs_ref[one, at] = jnp.sum(grad * w_v[group, at].astype(F32), axis=0, keepdims=True)
                gw_v[group, at] = (grad * (sc_ref[one, at] * mk_ref[one, at].astype(F32))).astype(BF)

        done = pl.ds(r0, r1_ - r0)
        outs.append(pltpu.make_async_copy(gw_v.at[done], gw_hbm.at[done], lsem.at[3 + i]))
        outs[-1].start()
    outs.append(pltpu.make_async_copy(gs_ref, gs_hbm, lsem.at[5]))
    outs[-1].start()
    for cp in outs:
        cp.wait()
    gh_out.wait()
    for group in sent:
        group.finish()


def hand_over(gh, gw, gs, gh_out, gw_out, gs_out, gh_v, gw_v, gs_v, sem):
    pieces = [(gw.at[at], gw_v.at[at], gw_out.at[at]) for at in (pl.ds(i * 208, 208) for i in range(8))]
    pieces += [(gh, gh_v, gh_out), (gs, gs_v, gs_out)]
    into = [pltpu.make_async_copy(a, b, sem.at[0, i]) for i, (a, b, _) in enumerate(pieces)]
    out = [pltpu.make_async_copy(b, c, sem.at[1, i]) for i, (_, b, c) in enumerate(pieces)]
    for cp in into:
        cp.start()
    for first, then in zip(into, out):
        first.wait()
        then.start()
    for cp in out:
        cp.wait()


def solution(mesh):
    def step(hidden, upstream, weight, scales, clip_mask, rot_block):
        s128 = jnp.asarray(sign_matrix(HB), BF)
        vmem = pl.BlockSpec(memory_space=pltpu.VMEM)
        smem = pl.BlockSpec(memory_space=pltpu.SMEM)
        anywhere = pl.BlockSpec(memory_space=pl.ANY)
        full = pltpu.VMEM((W, HB), BF)
        two = pltpu.VMEM((2, W, HB), BF)
        halves = pltpu.VMEM((2, W // 2, HB), BF)
        whole = pltpu.VMEM((W, E), BF)
        scratch = [
            pltpu.VMEM((HB, 8 * E), BF), whole, whole, pltpu.VMEM((8 * HB, E), BF), pltpu.VMEM((NC, HB, HB), F32),
            full, full, full, full, full, full, two, full, pltpu.VMEM((8, W, HB), BF),
            pltpu.VMEM((4, 2, W, HB), BF), two, pltpu.VMEM((2, 2, W, HB), BF), halves, halves, two,
            full, full, full, full, full, full, pltpu.VMEM((HB, W), BF), pltpu.VMEM((W, E), F32), whole,
            pltpu.VMEM((NC, E), F32), pltpu.SemaphoreType.DMA((N_SEM,)), pltpu.SemaphoreType.DMA((N_SEM,)), pltpu.SemaphoreType.DMA((8,)),
        ]
        shapes = (
            jax.ShapeDtypeStruct((HB, W), BF),
            jax.ShapeDtypeStruct((W, E), BF),
            jax.ShapeDtypeStruct((NC, E), F32),
        )
        results = pl.pallas_call(
            kernel,
            name="fused",
            out_shape=shapes,
            in_specs=[vmem, anywhere, anywhere, vmem, vmem, smem, vmem],
            out_specs=(anywhere,) * 3,
            scratch_shapes=scratch,
            compiler_params=pltpu.CompilerParams(
                collective_id=0, has_side_effects=True, vmem_limit_bytes=56 * 2**20
            ),
        )(hidden, upstream, weight, scales, clip_mask, rot_block, s128)
        return pl.pallas_call(
            hand_over,
            name="hand_over",
            out_shape=shapes,
            in_specs=[anywhere] * 3,
            out_specs=(anywhere,) * 3,
            scratch_shapes=[
                pltpu.VMEM((HB, W), BF), whole, pltpu.VMEM((NC, E), F32), pltpu.SemaphoreType.DMA((2, 10)),
            ],
        )(*results)

    return jax.shard_map(
        step,
        mesh=mesh,
        in_specs=(
            P("dp", "tensor"),
            P("dp", None),
            P("tensor", "dp"),
            P("tensor", "dp"),
            P("tensor", "dp"),
            P(),
        ),
        out_specs=(P("dp", "tensor"), P("tensor", "dp"), P("tensor", "dp")),
        check_vma=False,
    )
```

```python
import jax
import jax.numpy as jnp
import numpy as np
from jax import lax
from jax.experimental import pallas as pl
from jax.experimental.pallas import tpu as pltpu
from jax.sharding import PartitionSpec as P

MESH = pl.DeviceIdType.MESH
BF = jnp.bfloat16
F32 = jnp.float32
HB = 128
NC = 13
W = NC * HB
E = 1024
CHUNKS = ((0, 768), (768, 1664))
OUT_ROWS = ((0, 896), (896, 1664))
PLACE = {0: 0, 1: 256, 3: 512, 2: 768}
N_SEM = 40


def sign_matrix(size):
    table = np.ones((1, 1), np.float32)
    while table.shape[0] < size:
        table = np.block([[table, table], [table, -table]])
    return table


def rows(start, size, step):
    return pl.ds(pl.multiple_of(start, step), size)


def mix_blocks(first, store, coef):
    @pl.loop(0, 4)
    def _(i):
        at = rows(i * 32, 32, 32)
        parts = [first[k, at, :] for k in range(NC)]
        for o in range(NC):
            total = parts[0] * coef(0, o)
            for k in range(1, NC):
                total = total + parts[k] * coef(k, o)
            store(i, o, (total * HB**-0.5).astype(BF))


def kernel(
    h_ref, up_hbm, w_hbm, sc_ref, rot_ref, s128_ref,
    mixed_hbm, last_hbm, acc_hbm, up_out,
    up_v, w_v, wq, up, first, loc, loc_in, u, z_in, z_out, wz, xa, xa_send, rot,
    part, r1, r2, t_in, comp, x_in, g, g_in, gu, gz_in, gz_out, acc, acc_out,
    ssem, rsem, lsem,
):
    dp, tensor = lax.axis_index("dp"), lax.axis_index("tensor")
    xl, y = dp // 4, dp % 4
    z, xh, c = tensor // 4, (tensor // 2) % 2, tensor % 2
    sign_c = (1 - 2 * c).astype(F32)
    sign_x = (1 - 2 * xh).astype(F32)
    sent = []

    def y_dev(d):
        return (xl * 4 + (y + d) % 4, tensor)

    def x_dev(q, d=0):
        return ((1 - xl) * 4 + (y + d) % 4, z * 4 + ((xh + q) % 2) * 2 + c)

    def z_dev(k):
        return (dp, ((z + k) % 8) * 4 + xh * 2 + c)

    core_dev = (dp, z * 4 + xh * 2 + (1 - c))

    stores = []

    def store(src, dst):
        stores.append(pltpu.make_async_copy(src, dst, lsem.at[2 + len(stores)]))
        stores[-1].start()

    class Group:
        def __init__(self, like):
            self.like, self.i = like, len(sent)
            sent.append(self)

        def send(self, src, dst, dev):
            pltpu.make_async_remote_copy(
                src_ref=src, dst_ref=dst, send_sem=ssem.at[self.i], recv_sem=rsem.at[self.i],
                device_id=dev, device_id_type=MESH,
            ).start()
            return self

        def recv(self):
            pltpu.make_async_copy(self.like, self.like, rsem.at[self.i]).wait()

        def finish(self):
            pltpu.make_async_copy(self.like, self.like, ssem.at[self.i]).wait()

    def send(src, dst, dev):
        return Group(src).send(src, dst, dev)

    def wide(ref, *at):
        return ref[at].astype(F32)

    up_load = pltpu.make_async_copy(up_hbm, up_v, lsem.at[1])
    up_load.start()
    w_load = pltpu.make_async_copy(w_hbm, w_v, lsem.at[0])
    w_load.start()
    peers = [y_dev(d) for d in (1, 2, 3)] + [x_dev(q, d) for d in range(4) for q in range(2)]
    peers += [z_dev(k) for k in range(1, 8)] + [core_dev]
    barrier = pltpu.get_barrier_semaphore()
    for dev in peers:
        pl.semaphore_signal(barrier, inc=1, device_id=dev, device_id_type=MESH)

    for k in range(NC):
        first[k] = lax.dot_general(
            s128_ref[...], h_ref[:, k * HB : (k + 1) * HB], (((1,), (1,)), ((), ())),
            preferred_element_type=F32,
        )

    def store_loc(i, o, value):
        loc[rows(o * HB + i * 32, 32, 32), :] = value

    mix_blocks(first, store_loc, lambda k, o: rot_ref[k, o])
    up_load.wait()
    pl.semaphore_wait(barrier, len(peers))

    up_cp = {}
    def up_start(d):
        slot_of = (4 - d) % 4
        there = PLACE[slot_of]
        up_cp[slot_of] = Group(up.at[pl.ds(there, HB if d else 64)])
        if d:
            to = xl * 4 + (y + d) % 4
            up_cp[slot_of].send(
                up_v.at[rows(c * 64, 64, 64), pl.ds(pl.multiple_of(to * E, E), E)],
                up.at[rows(there + c * 64, 64, 64)],
                y_dev(d),
            )
        to = (1 - xl) * 4 + (y + d) % 4
        quarter = c * 64 + xh * 32
        for q in range(2):
            up_cp[slot_of].send(
                up_v.at[rows(quarter, 32, 32), pl.ds(pl.multiple_of(to * E, E), E)],
                up.at[rows(there + HB + quarter, 32, 32)],
                x_dev(q, d),
            )
    up_start(2)
    up_start(0)
    core_a = send(loc, loc_in, core_dev)

    def share_up(d):
        up_cp[d].recv()
        shared = Group(up.at[pl.ds(PLACE[d], HB if d else 64)])
        for xr in range(0 if d else 1, 2):
            block = up.at[rows(PLACE[d] + xr * HB + c * 64, 64, 64)]
            shared.send(block, block, core_dev)
        return shared

    w_load.wait()

    @pl.loop(0, NC)
    def _(i):
        at = rows(i * HB, HB, HB)
        wq[at, :] = (w_v[at, :].astype(F32) * sc_ref[pl.ds(i, 1), :]).astype(BF)

    def z_start(src, dst, r0, r1_):
        b = (r1_ - r0) // 8
        at = rows(r0 + z * b, b, 16)
        group = Group(dst.at[pl.ds(r0, 7 * b)])
        for k in (4, 3, 5, 2, 6, 1, 7):
            group.send(src.at[rows(r0 + ((z + k) % 8) * b, b, 16)], dst.at[at], z_dev(k))
        if dst is mixed_hbm:
            store(src.at[at], dst.at[at])
        else:
            dst[at, :] = src[at, :]
        return group

    def z_mix(src, dst, r0, r1_):
        b = (r1_ - r0) // 8

        @pl.loop(0, b // 16)
        def _(i):
            at = [rows(r0 + k * b + i * 16, 16, 16) for k in range(8)]
            v = [wide(src, at[k]) for k in range(8)]
            for bit in (1, 2, 4):
                v = [v[k ^ bit] - v[k] if k & bit else v[k] + v[k | bit] for k in range(8)]
            for k in range(8):
                dst[at[k], :] = (v[k] * 32.0**-0.5).astype(BF)

    core_a.recv()
    u[...] = (wide(loc, ...) * sign_c + wide(loc_in, ...)).astype(BF)
    za = [z_start(u, z_in, *rs) for rs in CHUNKS]
    up_start(1)
    up_start(3)

    def multiply(d):
        group = up[PLACE[d] : PLACE[d] + 256, :]
        r = lax.dot_general(wq[...], group, (((1,), (1,)), ((), ())), preferred_element_type=F32)
        for xr in range(2):
            part[d, xr] = r[:, xr * HB : (xr + 1) * HB].astype(BF)

    r1_cp, r2_cp = {}, {}

    def chunk(j):
        return pl.ds(CHUNKS[j][0], CHUNKS[j][1] - CHUNKS[j][0])

    def y_first(j):
        at = chunk(j)
        r1_cp[j] = [
            send(part.at[2, 0, at], r1.at[0, at], y_dev(1)),
            send(part.at[2, 1, at], r1.at[1, at], y_dev(3)),
        ]

    def y_direct(j):
        at = chunk(j)
        r2_cp[j] = Group(r2.at[:, :, at])
        r2_cp[j].send(part.at[1, 1, at], r2.at[0, 1, at], y_dev(1))
        r2_cp[j].send(part.at[3, 0, at], r2.at[1, 0, at], y_dev(3))

    def y_second(j):
        at = chunk(j)
        r1_cp[j][0].recv()
        part[1, 0, at] = (wide(part, 1, 0, at) + wide(r1, 0, at)).astype(BF)
        r2_cp[j].send(part.at[1, 0, at], r2.at[0, 0, at], y_dev(1))
        r1_cp[j][1].recv()
        part[3, 1, at] = (wide(part, 3, 1, at) + wide(r1, 1, at)).astype(BF)
        r2_cp[j].send(part.at[3, 1, at], r2.at[1, 1, at], y_dev(3))

    t_cp, x_cp, g_cp, gz_cp, gw_cp = {}, {}, {}, {}, {}

    def half(j, which):
        r0, r1_ = CHUNKS[j]
        return rows(r0 + which * ((r1_ - r0) // 2), (r1_ - r0) // 2, 64)

    def packed(j):
        r0, r1_ = CHUNKS[j]
        return pl.ds(r0 // 2, (r1_ - r0) // 2)

    def x_first(j):
        at = chunk(j)
        r2_cp[j].recv()
        for xr in range(2):
            total = wide(part, 0, xr, at) + wide(r2, 0, xr, at) + wide(r2, 1, xr, at)
            part[0, xr, at] = total.astype(BF)
        t_cp[j], x_cp[j] = Group(t_in.at[:, packed(j)]), Group(x_in.at[:, at])
        other = half(j, 1 - xh)
        for q in range(2):
            t_cp[j].send(part.at[0, 0, half(j, (xh + q) % 2)], t_in.at[q, packed(j)], x_dev(q))
        for q in range(2):
            x_cp[j].send(part.at[0, 1, other], x_in.at[q, other], x_dev(q))

    def x_second(j):
        mine, there = half(j, xh), packed(j)
        t_cp[j].recv()
        own = wide(part, 0, 1, mine)
        comp[0, there] = (own * sign_x + wide(t_in, 1, there)).astype(BF)
        comp[1, there] = (own + wide(t_in, 0, there)).astype(BF)
        for q in range(2):
            x_cp[j].send(comp.at[q, there], x_in.at[q, mine], x_dev(q))

    def core_first(j):
        x_cp[j].recv()
        near, far = half(j, xh), half(j, 1 - xh)
        g[near, :] = (wide(part, 0, 0, near) * sign_x + wide(x_in, 0, near) + wide(x_in, 1, near)).astype(BF)
        g[far, :] = ((wide(part, 0, 0, far) + wide(x_in, 0, far)) * sign_x + wide(x_in, 1, far)).astype(BF)
        g_cp[j] = send(g.at[chunk(j)], g_in.at[chunk(j)], core_dev)

    def core_second(j):
        at = chunk(j)
        g_cp[j].recv()
        gu[at, :] = (wide(g, at) * sign_c + wide(g_in, at)).astype(BF)
        gz_cp[j] = z_start(gu, gz_in, *CHUNKS[j])

    def z_second(j):
        gz_cp[j].recv()
        z_mix(gz_in, gz_out, *CHUNKS[j])
        gw_cp[j] = z_start(gz_out, mixed_hbm, *CHUNKS[j])

    def grad_step(slots, fresh=False):
        tokens = slice(slots[0] * HB, (slots[-1] + 1) * HB)
        for r0, r1_ in ((0, W // 2), (W // 2, W)):

            @pl.loop(0, 2)
            def _(i):
                columns = rows(i * 512, 512, 512)
                block = jnp.concatenate([rot[k, r0:r1_, :] for k in slots], axis=1)
                term = jnp.dot(block, up[tokens, columns], preferred_element_type=F32)
                if fresh:
                    acc[r0:r1_, columns] = term
                else:
                    acc_out[r0:r1_, columns] = (acc[r0:r1_, columns] + term).astype(BF)

    def slot(d, xr):
        return PLACE[d] // HB + xr

    def gather_first(xr):
        own = rot.at[slot(0, xr)]
        return send(own, rot.at[slot(3, xr)], y_dev(1)), send(own, rot.at[slot(1, xr)], y_dev(3))

    def gather_second(cps, xr):
        top, low = pl.ds(0, W // 2), pl.ds(W // 2, W // 2)
        cps[0].recv()
        one = send(rot.at[slot(3, xr), top], last_hbm.at[xr, top], y_dev(1))
        cps[1].recv()
        two = send(rot.at[slot(1, xr), low], last_hbm.at[xr, low], y_dev(3))
        return [one, two]

    zb = []
    def zret(j):
        za[j].recv()
        z_mix(z_in, z_out, *(CHUNKS[j] if len(za) == 2 else (0, W)))
        zb.append(z_start(z_out, wz, *(CHUNKS[j] if len(za) == 2 else (0, W))))
    xa_cp = Group(xa)
    def xa_start(j):
        zb[j].recv()
        at = chunk(j) if len(za) == 2 else pl.ds(0, W)
        for q in range(2):
            xa_cp.send(wz.at[at], xa.at[q, at], x_dev(q))
    def p0():
        shared.recv()
        up[0:HB, :] = up_v[:, pl.ds(pl.multiple_of(dp * E, E), E)]
        multiply(0)
    def xmid():
        xa_cp.recv()
        rot[slot(0, 1)] = (wide(xa, 0) * sign_x + wide(xa, 1)).astype(BF)
        xa_send[...] = (wide(xa, 0) - wide(xa, 1) * sign_x).astype(BF)
        own_half = rows(xh * (W // 2), W // 2, W // 2)
        xb_cp = Group(rot.at[slot(0, 0)])
        xb_cp.send(rot.at[slot(0, 1), own_half], rot.at[slot(0, 0), own_half], x_dev(0))
        xb_cp.send(xa_send.at[own_half], rot.at[slot(0, 0), own_half], x_dev(1))
        return xb_cp
    shared = share_up(2)
    shared.recv()
    multiply(2)
    y_first(0)
    store(up.at[pl.ds(PLACE[2], 256)], up_out)
    shared = share_up(1), share_up(3)
    shared[0].recv()
    shared[1].recv()
    multiply(1)
    multiply(3)
    y_direct(0)
    y_first(1)
    shared = share_up(0)
    for j in range(len(za)): zret(j)
    p0()
    y_second(0)
    y_direct(1)
    for j in range(len(za)): xa_start(j)
    x_first(0)
    y_second(1)
    x_second(0)
    xb_cp = xmid()
    far_cp = gather_first(1)
    core_first(0)
    core_second(0)
    x_first(1)
    xb_cp.recv()
    near_cp = gather_first(0)
    x_second(1)
    z_second(0)
    last = gather_second(far_cp, 1)
    core_first(1)
    core_second(1)
    grad_step((0, 1), True)
    z_second(1)
    last += gather_second(near_cp, 0)
    grad_step((2, 3, 4, 5))
    store(acc_out, acc_hbm)
    gw_cp[0].recv()
    gw_cp[1].recv()
    for cp in last:
        cp.recv()
    for cp in stores:
        cp.wait()
    for group in sent:
        group.finish()


def finish(
    mixed_hbm, last_hbm, acc_hbm, up_hbm, w_hbm, sc_ref, mk_ref, rot_ref, s128_ref,
    gh_hbm, gw_hbm, gs_hbm,
    mixed, last, acc, up, w_v, first, gh_v, grad_v, gw_v, gs_v, sem,
):
    started = []

    def copy(src, dst):
        cp = pltpu.make_async_copy(src, dst, sem.at[len(started)])
        started.append(cp)
        cp.start()
        return cp

    head = copy(mixed_hbm, mixed), copy(last_hbm, last), copy(up_hbm, up)
    loads = []
    for r0, r1_ in OUT_ROWS:
        at = pl.ds(r0, r1_ - r0)
        loads.append((copy(acc_hbm.at[at], acc.at[at]), copy(w_hbm.at[at], w_v.at[at])))
    head[0].wait()
    for k in range(NC):
        first[k] = lax.dot_general(
            mixed[k * HB : (k + 1) * HB, :], s128_ref[...], (((0,), (0,)), ((), ())),
            preferred_element_type=F32,
        )

    def store_gh(i, o, value):
        gh_v[rows(i * 32, 32, 32), o * HB : (o + 1) * HB] = value

    mix_blocks(first, store_gh, lambda k, o: rot_ref[o, k])
    out = [copy(gh_v, gh_hbm)]
    head[1].wait()
    head[2].wait()
    for (r0, r1_), (one, two) in zip(OUT_ROWS, loads):
        one.wait()

        @pl.loop(0, 2)
        def _(i):
            columns = rows(i * 512, 512, 512)
            block = jnp.concatenate([last[k, r0:r1_, :] for k in range(2)], axis=1)
            term = jnp.dot(block, up[:, columns], preferred_element_type=F32)
            grad_v[r0:r1_, columns] = term + acc[r0:r1_, columns].astype(F32)

        two.wait()

        @pl.loop(r0 // HB, r1_ // HB)
        def _(k):
            group = rows(k * HB, HB, HB)
            one = pl.ds(k, 1)
            for at in (slice(0, 512), slice(512, 1024)):
                grad = grad_v[group, at]
                gs_v[one, at] = jnp.sum(grad * w_v[group, at].astype(F32), axis=0, keepdims=True)
                gw_v[group, at] = (grad * (sc_ref[one, at] * mk_ref[one, at].astype(F32))).astype(BF)

        done = pl.ds(r0, r1_ - r0)
        out.append(copy(gw_v.at[done], gw_hbm.at[done]))
    out.append(copy(gs_v, gs_hbm))
    for cp in out:
        cp.wait()


def solution(mesh):
    def step(hidden, upstream, weight, scales, clip_mask, rot_block):
        s128 = jnp.asarray(sign_matrix(HB), BF)
        vmem = pl.BlockSpec(memory_space=pltpu.VMEM)
        smem = pl.BlockSpec(memory_space=pltpu.SMEM)
        anywhere = pl.BlockSpec(memory_space=pl.ANY)
        full = pltpu.VMEM((W, HB), BF)
        two = pltpu.VMEM((2, W, HB), BF)
        halves = pltpu.VMEM((2, W // 2, HB), BF)
        whole = pltpu.VMEM((W, E), BF)
        first = pltpu.VMEM((NC, HB, HB), F32)
        scratch = [
            pltpu.VMEM((HB, 8 * E), BF), whole, whole, pltpu.VMEM((8 * HB, E), BF), first,
            full, full, full, full, full, full, two, full, pltpu.VMEM((6, W, HB), BF),
            pltpu.VMEM((4, 2, W, HB), BF), two, pltpu.VMEM((2, 2, W, HB), BF), halves, halves, two,
            full, full, full, full, full, pltpu.VMEM((W, E), F32), whole,
            pltpu.SemaphoreType.DMA((N_SEM,)), pltpu.SemaphoreType.DMA((N_SEM,)), pltpu.SemaphoreType.DMA((8,)),
        ]
        mixed, last, acc, up = pl.pallas_call(
            kernel,
            name="exchange",
            out_shape=(
                jax.ShapeDtypeStruct((W, HB), BF),
                jax.ShapeDtypeStruct((2, W, HB), BF),
                jax.ShapeDtypeStruct((W, E), BF),
                jax.ShapeDtypeStruct((2 * HB, E), BF),
            ),
            in_specs=[vmem, anywhere, anywhere, vmem, smem, vmem],
            out_specs=(anywhere,) * 4,
            scratch_shapes=scratch,
            compiler_params=pltpu.CompilerParams(
                collective_id=0, has_side_effects=True, vmem_limit_bytes=56 * 2**20
            ),
        )(hidden, upstream, weight, scales, rot_block, s128)
        return pl.pallas_call(
            finish,
            name="finish",
            out_shape=(
                jax.ShapeDtypeStruct((HB, W), BF),
                jax.ShapeDtypeStruct((W, E), BF),
                jax.ShapeDtypeStruct((NC, E), F32),
            ),
            in_specs=[anywhere] * 5 + [vmem, vmem, smem, vmem],
            out_specs=(anywhere,) * 3,
            scratch_shapes=[
                full, two, whole, pltpu.VMEM((2 * HB, E), BF), whole, first,
                pltpu.VMEM((HB, W), BF), pltpu.VMEM((W, E), F32), whole, pltpu.VMEM((NC, E), F32),
                pltpu.SemaphoreType.DMA((16,)),
            ],
            compiler_params=pltpu.CompilerParams(vmem_limit_bytes=56 * 2**20),
        )(mixed, last, acc, up, weight, scales, clip_mask, rot_block, s128)

    return jax.shard_map(
        step,
        mesh=mesh,
        in_specs=(
            P("dp", "tensor"),
            P("dp", None),
            P("tensor", "dp"),
            P("tensor", "dp"),
            P("tensor", "dp"),
            P(),
        ),
        out_specs=(P("dp", "tensor"), P("tensor", "dp"), P("tensor", "dp")),
        check_vma=False,
    )
```
